256 devices in a mesh: grp: 4 (over x), seq: 64 (over z, y, core).
Axes of the slice: x: 4, y: 4, z: 8, core: 2. Of those that a mesh axis runs over, the one named last changes fastest.
Arguments:
- queries: bfloat16 [4, 16384, 4096], P('grp', 'seq'), may hold values from -6 to 6
- key_base: bfloat16 [4, 16384, 512], P('grp', 'seq'), may hold values from -6 to 6
- value_base: bfloat16 [4, 16384, 512], P('grp', 'seq'), may hold values from -6 to 6
- out_grad: bfloat16 [4, 16384, 4096], P('grp', 'seq'), may hold values from -6 to 6
- doc_lengths: int32 [4, 128], P('grp'), may hold values from 1 to 512, 16384 in all within a row
- key_scale: float32 [512], replicated, may hold values from 0.5 to 1.5
- value_scale: float32 [512], replicated, may hold values from 0.5 to 1.5
Outputs:
- grad_queries: bfloat16 [4, 16384, 4096], P('grp', 'seq')
- grad_key_base: bfloat16 [4, 16384, 512], P('grp', 'seq')
- grad_value_base: bfloat16 [4, 16384, 512], P('grp', 'seq')
- grad_key_scale: float32 [512], replicated
- grad_value_scale: float32 [512], replicated
The draws below stay inside these ranges and needn't reach their ends.
Inputs may be any that keep to these rules, and one draw needn't show every extreme that they name: `doc_lengths`: the lengths of one packed sequence sum to 16384; the largest is exactly 512.
All inputs are finite; a program needn't handle non-finite values.
Results may differ from the reference program's by a relative error of at most 0.012.
The reference program's roundings to bfloat16 on the way (of `keys`, `values`, `probs` and `dscores`) count: a program that leaves them out, or rounds other values in their place, can miss the bound.
Values may be sent and summed in bfloat16 or wider, within the bound.
No kernel may reach another device: no remote copies, remote signals or barrier semaphores. Data moves between devices by JAX's collectives and lax.ppermute only.
A program may use at most 128 MiB of HBM per device.

```python
import math
import jax
import jax.numpy as jnp
import numpy as np
from jax import lax

QH = 32
KVH = 4
HD = 128
TOK_DEV = 256
DOC_MOST = 512
REACH = 2
TOKENS = 16384
DOCS = 128
N_GRP = 4


def draw_queries(key, part):
    key = jax.random.fold_in(key, 11)
    values = jax.random.normal(key, (N_GRP, TOKENS, QH * HD), jnp.float32)
    return jnp.clip(values, -6.0, 6.0).astype(jnp.bfloat16)


def draw_key_base(key, part):
    key = jax.random.fold_in(key, 23)
    values = jax.random.normal(key, (N_GRP, TOKENS, KVH * HD), jnp.float32)
    return jnp.clip(values, -6.0, 6.0).astype(jnp.bfloat16)


def block_levels(own_key, shape, cuts, smallest, largest):
    factor_of, own = 1.0, jax.random.fold_in(own_key, 6)
    for dim, parts in cuts:
        draws = jnp.exp(jax.random.uniform(jax.random.fold_in(own, dim), (parts,), jnp.float32, smallest / len(cuts), largest / len(cuts)))
        factor_of = factor_of * jnp.repeat(draws, shape[dim] // parts).reshape([-1 if axis == dim else 1 for axis in range(len(shape))])
    return factor_of


def split_up(number_of, total, most, skew):
    loads = [(1 << 20) // math.isqrt(standing ** skew) + 1 for standing in range(2, number_of + 1)]
    surplus, holding = total - most - (number_of - 1), [1] * (number_of - 1)
    while surplus > 0:
        candidates = [i for i in range(number_of - 1) if holding[i] < most]
        mass, left = sum([loads[i] for i in candidates]), surplus
        for i in candidates:
            extra = min(most - holding[i], max(1, left * loads[i] // mass), surplus)
            holding[i] = holding[i] + extra
            surplus = surplus - extra
    return np.array([most] + holding)


def ragged_sizes(stream_key, count, total, most, lean):
    if count == 2:
        one = jax.random.randint(stream_key, (), max(1, total - most), min(most, total - 1) + 1)
        return jnp.stack([one, total - one])
    tallies = jnp.asarray(split_up(count, total, most, lean), jnp.int32)
    twos = (count - 1) // 2
    donor, taker = tallies[1:1 + 2 * twos:2], tallies[2:2 + 2 * twos:2]
    slack = jnp.minimum(donor - 1, most - taker)
    moved = jax.random.randint(jax.random.fold_in(stream_key, 1), (twos,), 0, 1 << 20) % (slack + 1)
    tallies = tallies.at[1:1 + 2 * twos:2].set(donor - moved).at[2:2 + 2 * twos:2].set(taker + moved)
    return tallies[jax.random.permutation(jax.random.fold_in(stream_key, 2), count)]


def centred(stream_key, extent, spread, reach, cuts=(), held_as=jnp.bfloat16):
    result = jax.random.normal(stream_key, extent, jnp.float32) * spread
    if len(cuts) > 0:
        result = block_levels(stream_key, extent, cuts, -0.22, 0.18) * result
    return jnp.clip(result, min=-reach, max=reach).astype(held_as)


def setup_inputs(seed: int = 0) -> dict:
    streams_of = jax.random.split(jax.random.key(seed), 8)
    queries = draw_queries(jax.random.fold_in(streams_of[7], 71), 0)
    key_base = draw_key_base(jax.random.fold_in(streams_of[7], 71), 0)
    value_base = centred(streams_of[2], (N_GRP, TOKENS, KVH * HD), 1.0, 6.0, ((0, 4), (1, 64)))
    out_grad = centred(streams_of[3], (N_GRP, TOKENS, QH * HD), 1.0, 6.0, ((0, 4), (1, 64)))
    doc_lengths = jax.vmap(lambda own: ragged_sizes(own, DOCS, TOKENS, DOC_MOST, 2))(jax.random.split(streams_of[4], N_GRP)).reshape((N_GRP, DOCS)).astype(jnp.int32)
    key_scale = jnp.clip(1.0 + 0.1 * jax.random.normal(streams_of[5], (KVH * HD,), jnp.float32), 0.5, 1.5)
    value_scale = jnp.clip(1.0 + 0.1 * jax.random.normal(streams_of[6], (KVH * HD,), jnp.float32), 0.5, 1.5)
    return {"queries": queries, "key_base": key_base, "value_base": value_base, "out_grad": out_grad, "doc_lengths": doc_lengths, "key_scale": key_scale, "value_scale": value_scale}


def head_backward(q_part, grad_part, key_part, value_part, allowed):
    inv_root = 1.0 / math.sqrt(HD)
    qf = q_part.astype(jnp.float32)
    gf = grad_part.astype(jnp.float32)
    kf = key_part.astype(jnp.float32)
    vf = value_part.astype(jnp.float32)
    scores = jnp.einsum('tgd,kd->gtk', qf, kf) * inv_root
    scores = jnp.where(allowed[None], scores, jnp.float32(-1e+30))
    row_max = lax.optimization_barrier(jnp.max(scores, axis=-1))
    log_total = row_max + jnp.log(lax.optimization_barrier(jnp.sum(jnp.exp(scores - row_max[..., None]), axis=-1)))
    weights = jnp.exp(scores - log_total[..., None])
    probs = lax.optimization_barrier(weights.astype(jnp.bfloat16)).astype(jnp.float32)
    attn_out = jnp.einsum('gtk,kd->tgd', probs, vf)
    delta = lax.optimization_barrier(jnp.sum(gf * attn_out, axis=-1))
    dprobs = jnp.einsum('tgd,kd->gtk', gf, vf)
    dscores = weights * (dprobs - delta.T[:, :, None])
    dscores = lax.optimization_barrier(dscores.astype(jnp.bfloat16)).astype(jnp.float32)
    grad_q = jnp.einsum('gtk,kd->tgd', dscores, kf) * inv_root
    grad_k = jnp.einsum('gtk,tgd->kd', dscores, qf) * inv_root
    grad_v = jnp.einsum('gtk,tgd->kd', probs, gf)
    return (grad_q, grad_k, grad_v)

def reference(queries, key_base, value_base, out_grad, doc_lengths, key_scale, value_scale):
    width = KVH * HD
    per_group = QH // KVH
    span = (REACH + 1) * TOK_DEV
    front = REACH * TOK_DEV
    grads_q = []
    grads_k = []
    grads_v = []
    key_total = jnp.zeros((width,), jnp.float32)
    value_total = jnp.zeros((width,), jnp.float32)
    for seqno in range(N_GRP):
        lengths = doc_lengths[seqno]
        starts = jnp.cumsum(lengths) - lengths
        positions = jnp.arange(TOKENS, dtype=jnp.int32)
        doc_start = lax.optimization_barrier(jnp.max(jnp.where(starts[None, :] <= positions[:, None], starts[None, :], 0), axis=1)).astype(jnp.int32)
        keys = (key_base[seqno].astype(jnp.float32) * key_scale).astype(jnp.bfloat16)
        values = (value_base[seqno].astype(jnp.float32) * value_scale).astype(jnp.bfloat16)
        keys_pad = jnp.concatenate([jnp.zeros((front, width), jnp.bfloat16), keys], axis=0)
        values_pad = jnp.concatenate([jnp.zeros((front, width), jnp.bfloat16), values], axis=0)
        q_seq = queries[seqno]
        g_seq = out_grad[seqno]

        def block_step(carry, block):
            dk_pad, dv_pad = carry
            first = (block * TOK_DEV).astype(jnp.int32)
            q_block = lax.dynamic_slice_in_dim(q_seq, first, TOK_DEV, 0)
            g_block = lax.dynamic_slice_in_dim(g_seq, first, TOK_DEV, 0)
            k_window = lax.dynamic_slice_in_dim(keys_pad, first, span, 0)
            v_window = lax.dynamic_slice_in_dim(values_pad, first, span, 0)
            q_pos = first + jnp.arange(TOK_DEV, dtype=jnp.int32)
            k_pos = first - front + jnp.arange(span, dtype=jnp.int32)
            d_start = lax.dynamic_slice_in_dim(doc_start, first, TOK_DEV, 0)
            allowed = (k_pos[None, :] >= d_start[:, None]) & (k_pos[None, :] <= q_pos[:, None])
            parts_q = []
            parts_k = []
            parts_v = []
            for head in range(KVH):
                lo = head * per_group * HD
                hi = (head + 1) * per_group * HD
                q_part = q_block[:, lo:hi].reshape(TOK_DEV, per_group, HD)
                g_part = g_block[:, lo:hi].reshape(TOK_DEV, per_group, HD)
                grad_q, grad_k, grad_v = head_backward(q_part, g_part, k_window[:, head * HD:(head + 1) * HD], v_window[:, head * HD:(head + 1) * HD], allowed)
                parts_q.append(grad_q.reshape(TOK_DEV, per_group * HD))
                parts_k.append(grad_k)
                parts_v.append(grad_v)
            dk_block = jnp.concatenate(parts_k, axis=1)
            dv_block = jnp.concatenate(parts_v, axis=1)
            zero = jnp.int32(0)
            dk_pad = lax.dynamic_update_slice(dk_pad, lax.dynamic_slice(dk_pad, (first, zero), (span, width)) + dk_block, (first, zero))
            dv_pad = lax.dynamic_update_slice(dv_pad, lax.dynamic_slice(dv_pad, (first, zero), (span, width)) + dv_block, (first, zero))
            return ((dk_pad, dv_pad), jnp.concatenate(parts_q, axis=1))
        init = (jnp.zeros((front + TOKENS, width), jnp.float32), jnp.zeros((front + TOKENS, width), jnp.float32))
        (dk_pad, dv_pad), dq_blocks = lax.scan(block_step, init, jnp.arange(TOKENS // TOK_DEV, dtype=jnp.int32))
        grads_q.append(dq_blocks.reshape(TOKENS, QH * HD).astype(jnp.bfloat16))
        grad_keys = dk_pad[front:]
        grad_values = dv_pad[front:]
        grads_k.append((grad_keys * key_scale).astype(jnp.bfloat16))
        grads_v.append((grad_values * value_scale).astype(jnp.bfloat16))
        key_total = key_total + lax.optimization_barrier(jnp.sum(grad_keys * key_base[seqno].astype(jnp.float32), axis=0))
        value_total = value_total + lax.optimization_barrier(jnp.sum(grad_values * value_base[seqno].astype(jnp.float32), axis=0))
    norm = math.sqrt(N_GRP * TOKENS)
    return (jnp.stack(grads_q), jnp.stack(grads_k), jnp.stack(grads_v), key_total / norm, value_total / norm)
```

```python
import functools
import math

import jax
import jax.numpy as jnp
from jax import lax
from jax.experimental import pallas as pl
from jax.experimental.pallas import tpu as pltpu
from jax.sharding import PartitionSpec as P

HD = 128
REACH = 2
DOC_MOST = 512
QT = 128
KG = 128
LANES = 256
NEG = -1e30
F32 = jnp.float32
BF16 = jnp.bfloat16


def attend_kernel(
    info, dstart, kscale, vscale, q_ref, g_ref, k_own, v_own, far, near_a, near_b,
    dq_ref, own_ref, part_ref, sums_ref, bias, k_raw, v_raw, k_win, v_win, dk_acc, dv_acc,
):
    tok = k_own.shape[0]
    front = REACH * tok
    per_group = q_ref.shape[1] // HD
    packed = LANES // QT
    tiles = tok // QT
    most = (DOC_MOST + QT) // KG
    inv_root = 1.0 / math.sqrt(HD)
    log2_scale = inv_root * math.log2(math.e)

    @pl.when(pl.program_id(0) == 0)
    def _():
        k_pos = lax.broadcasted_iota(jnp.int32, (front + tok, LANES), 0)
        lane = lax.broadcasted_iota(jnp.int32, (front + tok, LANES), 1) % QT
        for tile in range(tiles):
            start = dstart[tile : tile + 1, :]
            q_pos = lane + (front + tile * QT)
            ok = (k_pos >= start) & (k_pos <= q_pos)
            bias[tile] = jnp.where(ok, 0.0, NEG)

    even = info[tiles] == 0
    k_raw[:tok] = far[:, :HD]
    v_raw[:tok] = far[:, HD:]
    near = jnp.where(even, near_b[...], near_a[...])
    k_raw[tok:front] = near[:, :HD]
    v_raw[tok:front] = near[:, HD:]
    k_raw[front:] = k_own[...]
    v_raw[front:] = v_own[...]
    k_win[...] = (k_raw[...].astype(F32) * kscale[...]).astype(BF16)
    v_win[...] = (v_raw[...].astype(F32) * vscale[...]).astype(BF16)
    dk_acc[...] = jnp.zeros_like(dk_acc)
    dv_acc[...] = jnp.zeros_like(dv_acc)

    nt = (((1,), (1,)), ((), ()))

    def one_tile(tile, units):
        row = pl.multiple_of(tile * QT, QT)
        count = units * KG
        low = pl.multiple_of(front + (tile + 1) * QT - count, KG)
        rows = pl.ds(low, count)
        keys = k_win[rows, :]
        values = v_win[rows, :]
        keys_t = keys.T
        mask = bias[tile, rows, :]
        dk = None
        dv = None
        for first in range(0, per_group, packed):
            cols = [slice((first + i) * HD, (first + i + 1) * HD) for i in range(packed)]
            q_part = jnp.concatenate([q_ref[pl.ds(row, QT), c] for c in cols], axis=0)
            g_part = jnp.concatenate([g_ref[pl.ds(row, QT), c] for c in cols], axis=0)
            scores = lax.dot_general(keys, q_part, nt, preferred_element_type=F32)
            dprobs = lax.dot_general(values, g_part, nt, preferred_element_type=F32)
            scores = scores * log2_scale + mask
            peak = jnp.max(scores, axis=0, keepdims=True)
            raised = jnp.exp2(scores - peak)
            inverse = 1.0 / jnp.sum(raised, axis=0, keepdims=True)
            weights = raised * inverse
            delta = jnp.sum(weights * dprobs, axis=0, keepdims=True)
            probs = weights.astype(BF16)
            dscores = (weights * (dprobs - delta)).astype(BF16)
            dv_one = jnp.dot(probs, g_part, preferred_element_type=F32)
            dk_one = jnp.dot(dscores, q_part, preferred_element_type=F32)
            dv = dv_one if dv is None else dv + dv_one
            dk = dk_one if dk is None else dk + dk_one
            dq_t = jnp.dot(keys_t, dscores, preferred_element_type=F32) * inv_root
            dq = dq_t.T.astype(BF16)
            for i, c in enumerate(cols):
                dq_ref[pl.ds(row, QT), c] = dq[i * QT : (i + 1) * QT]
        dk_acc[rows, :] += dk
        dv_acc[rows, :] += dv

    def tile_step(tile, carry):
        units = info[tile]
        for static in range(1, most + 1):
            pl.when(units == static)(functools.partial(one_tile, tile, static))
        return carry

    lax.fori_loop(0, tiles, tile_step, 0)
    dk = dk_acc[...] * inv_root
    dv = dv_acc[...]
    own_ref[:, :HD] = dk[front:]
    own_ref[:, HD:] = dv[front:]
    part_ref[:, :HD] = dk[:front].astype(BF16)
    part_ref[:, HD:] = dv[:front].astype(BF16)
    sums_ref[0, 0:1, :] = jnp.sum(dk * k_raw[...].astype(F32), axis=0, keepdims=True)
    sums_ref[0, 1:2, :] = jnp.sum(dv * v_raw[...].astype(F32), axis=0, keepdims=True)


def attend(heads, first, info, dstart, kscale, vscale, q, g, k_own, v_own, far, near_a, near_b):
    tok = k_own.shape[0]
    span = (REACH + 1) * tok
    group = q.shape[1] * HD // k_own.shape[1]
    tiles = tok // QT

    def at(width, offset):
        return pl.BlockSpec((tok, width), lambda h: (0, h + offset))

    vec = pl.BlockSpec((1, HD), lambda h: (0, h + first))
    out_shape = (
        jax.ShapeDtypeStruct((tok, heads * group), BF16),
        jax.ShapeDtypeStruct((tok, heads * 2 * HD), F32),
        jax.ShapeDtypeStruct((REACH * tok, heads * 2 * HD), BF16),
        jax.ShapeDtypeStruct((heads, 2, HD), F32),
    )
    return pl.pallas_call(
        attend_kernel,
        grid=(heads,),
        in_specs=[
            pl.BlockSpec(memory_space=pltpu.SMEM),
            pl.BlockSpec((tiles, LANES), lambda h: (0, 0)),
            vec,
            vec,
            at(group, first),
            at(group, first),
            at(HD, first),
            at(HD, first),
            at(2 * HD, 0),
            at(2 * HD, 0),
            at(2 * HD, 0),
        ],
        out_specs=(
            at(group, 0),
            at(2 * HD, 0),
            pl.BlockSpec((REACH * tok, 2 * HD), lambda h: (0, h)),
            pl.BlockSpec((1, 2, HD), lambda h: (h, 0, 0)),
        ),
        out_shape=out_shape,
        scratch_shapes=[
            pltpu.VMEM((tiles, span, LANES), F32),
            pltpu.VMEM((span, HD), BF16),
            pltpu.VMEM((span, HD), BF16),
            pltpu.VMEM((span, HD), BF16),
            pltpu.VMEM((span, HD), BF16),
            pltpu.VMEM((span, HD), F32),
            pltpu.VMEM((span, HD), F32),
        ],
        compiler_params=pltpu.CompilerParams(vmem_limit_bytes=40 * 2**20),
        cost_estimate=pl.CostEstimate(
            flops=heads * 8 * 256 * 576 * 128 * 10, bytes_accessed=heads * 2**21, transcendentals=0
        ),
    )(info, dstart, kscale, vscale, q, g, k_own, v_own, far, near_a, near_b)


def total_over_devices(value):
    size = lax.axis_size("seq")
    for bit in (1, 2, 4, 8, 16, 32):
        value = value + lax.ppermute(value, "seq", [(i, i ^ bit) for i in range(size)])
    for bit in (1, 2):
        value = value + lax.ppermute(value, "grp", [(i, i ^ bit) for i in range(4)])
    return value


def body(queries, key_base, value_base, out_grad, doc_lengths, key_scale, value_scale):
    tok = queries.shape[1]
    size = lax.axis_size("seq")
    heads = key_base.shape[2] // HD
    k_own = key_base[0]
    v_own = value_base[0]
    to_odd = [(i, i + 1) for i in range(0, size, 2)]
    to_even = [(i + 1, i) for i in range(0, size, 2)]
    forward = [(i, i + 2) for i in range(size - 2)]
    backward = [(i + 2, i) for i in range(size - 2)]
    device_pos = lax.axis_index("seq")
    parity = device_pos % 2

    mine = jnp.stack([k_own.reshape(tok, heads, HD), v_own.reshape(tok, heads, HD)], axis=2)
    mine = mine.reshape(tok, heads * 2 * HD)
    far = lax.ppermute(mine, "seq", forward)
    near_a = lax.ppermute(mine, "seq", to_odd)
    near_b = lax.ppermute(far, "seq", to_even)

    lengths = doc_lengths[0]
    starts = jnp.cumsum(lengths) - lengths
    first_key = (device_pos - REACH) * tok
    q_pos = device_pos * tok + jnp.arange(tok, dtype=jnp.int32)
    doc_start = jnp.max(jnp.where(starts[None, :] <= q_pos[:, None], starts[None, :], 0), axis=1)
    rel = (doc_start - first_key).reshape(tok // QT, QT)
    ends = REACH * tok + (jnp.arange(tok // QT, dtype=jnp.int32) + 1) * QT
    units = jnp.clip((ends - rel[:, 0] + KG - 1) // KG, 1, (DOC_MOST + QT) // KG)
    info = jnp.concatenate([units, parity[None]]).astype(jnp.int32)
    dstart = jnp.tile(rel, (1, LANES // QT))

    dq, own, part, sums = attend(
        heads, 0, info, dstart, key_scale[None], value_scale[None], queries[0], out_grad[0],
        k_own, v_own, far, near_a, near_b,
    )
    totals = total_over_devices(sums)
    two_back = part[:tok]
    one_back = part[tok:]
    from_odd = lax.ppermute(one_back, "seq", to_even)
    to_prev = lax.ppermute(two_back, "seq", backward)
    even_to_odd = lax.ppermute(one_back, "seq", [(i + 1, i) for i in range(1, size - 1, 2)])
    own = own + from_odd.astype(F32) + to_prev.astype(F32) + even_to_odd.astype(F32)
    own = own.reshape(tok, heads, 2, HD)
    grad_key_base = (own[:, :, 0].reshape(tok, heads * HD) * key_scale).astype(BF16)
    grad_value_base = (own[:, :, 1].reshape(tok, heads * HD) * value_scale).astype(BF16)
    norm = math.sqrt(lax.axis_size("grp") * size * tok)
    return (
        dq[None],
        grad_key_base[None],
        grad_value_base[None],
        totals[:, 0].reshape(heads * HD) / norm,
        totals[:, 1].reshape(heads * HD) / norm,
    )


def solution(mesh):
    return jax.shard_map(
        body,
        mesh=mesh,
        in_specs=(
            P("grp", "seq", None),
            P("grp", "seq", None),
            P("grp", "seq", None),
            P("grp", "seq", None),
            P("grp", None),
            P(),
            P(),
        ),
        out_specs=(P("grp", "seq", None), P("grp", "seq", None), P("grp", "seq", None), P(), P()),
        check_vma=False,
    )
```

```python
import functools
import math

import jax
import jax.numpy as jnp
from jax import lax
from jax.experimental import pallas as pl
from jax.experimental.pallas import tpu as pltpu
from jax.sharding import PartitionSpec as P

HD = 128
REACH = 2
DOC_MOST = 512
QT = 64
KG = 64
LANES = 256
HEADS_STEP = 2
NEG = -1e30
F32 = jnp.float32
BF16 = jnp.bfloat16
NT = (((1,), (1,)), ((), ()))


def attend_kernel(
    info, dstart, kscale, vscale, q_ref, g_ref, k_own, v_own,
    far_k, far_v, near_ka, near_va, near_kb, near_vb,
    dq_ref, own_ref, two_ref, one_ref, sums_ref,
    bias, k_raw, v_raw, k_win, v_win, dk_acc, dv_acc,
):
    tok, width = k_own.shape
    heads = width // HD
    front = REACH * tok
    per_group = q_ref.shape[1] // width
    packed = LANES // QT
    parts = per_group // packed
    tiles = tok // QT
    most = (DOC_MOST + QT) // KG
    inv_root = 1.0 / math.sqrt(HD)
    log2_scale = inv_root * math.log2(math.e)

    @pl.when(pl.program_id(0) == 0)
    def _():
        reach = front + QT
        k_pos = lax.broadcasted_iota(jnp.int32, (reach, LANES), 0)
        lane = lax.broadcasted_iota(jnp.int32, (reach, LANES), 1) % QT
        for tile in range(tiles):
            start = dstart[tile : tile + 1, :] - tile * QT
            ok = (k_pos >= start) & (k_pos <= lane + front)
            bias[tile] = jnp.where(ok, 0.0, NEG)

    even = info[tiles] == 0
    for head in range(heads):
        cols = slice(head * HD, (head + 1) * HD)
        k_raw[head, :tok] = far_k[:, cols]
        v_raw[head, :tok] = far_v[:, cols]
        k_raw[head, tok:front] = jnp.where(even, near_kb[:, cols], near_ka[:, cols])
        v_raw[head, tok:front] = jnp.where(even, near_vb[:, cols], near_va[:, cols])
        k_raw[head, front:] = k_own[:, cols]
        v_raw[head, front:] = v_own[:, cols]
        k_win[head] = (k_raw[head].astype(F32) * kscale[:, cols]).astype(BF16)
        v_win[head] = (v_raw[head].astype(F32) * vscale[:, cols]).astype(BF16)
    dk_acc[...] = jnp.zeros_like(dk_acc)
    dv_acc[...] = jnp.zeros_like(dv_acc)

    def one_tile(tile, units):
        row = pl.multiple_of(tile * QT, QT)
        count = units * KG
        low = pl.multiple_of(front + (tile + 1) * QT - count, KG)
        rows = pl.ds(low, count)
        mask = bias[tile, front + QT - count :, :]

        def begin(group):
            head = group // parts
            at = range(group * packed, (group + 1) * packed)
            cols = [slice(c * HD, (c + 1) * HD) for c in at]
            q_part = jnp.concatenate([q_ref[pl.ds(row, QT), c] for c in cols], axis=0)
            g_part = jnp.concatenate([g_ref[pl.ds(row, QT), c] for c in cols], axis=0)
            scores = lax.dot_general(k_win[head, rows, :], q_part, NT, preferred_element_type=F32)
            dprobs = lax.dot_general(v_win[head, rows, :], g_part, NT, preferred_element_type=F32)
            return q_part, g_part, scores, dprobs

        def middle(q_part, g_part, scores, dprobs):
            scores = scores * log2_scale + mask
            peak = jnp.max(scores, axis=0, keepdims=True)
            raised = jnp.exp2(scores - peak)
            inverse = 1.0 / jnp.sum(raised, axis=0, keepdims=True)
            delta = jnp.sum(raised * dprobs, axis=0, keepdims=True) * inverse
            weights = raised * inverse
            probs = weights.astype(BF16)
            dscores = (weights * (dprobs - delta)).astype(BF16)
            return q_part, g_part, probs, dscores

        totals = [None] * heads

        def finish(group, q_part, g_part, probs, dscores):
            head = group // parts
            dv = jnp.dot(probs, g_part, preferred_element_type=F32)
            dk = jnp.dot(dscores, q_part, preferred_element_type=F32)
            if totals[head] is not None:
                dk = dk + totals[head][0]
                dv = dv + totals[head][1]
            totals[head] = (dk, dv)
            keys_t = k_win[head, rows, :].T
            dq_t = jnp.dot(keys_t, dscores, preferred_element_type=F32) * inv_root
            dq = dq_t.T.astype(BF16)
            for i in range(packed):
                c = (group * packed + i) * HD
                dq_ref[pl.ds(row, QT), c : c + HD] = dq[i * QT : (i + 1) * QT]
            if group % parts == parts - 1:
                dk_acc[head, rows, :] += dk
                dv_acc[head, rows, :] += dv

        groups = heads * parts
        begun = begin(0)
        done = None
        for group in range(groups):
            following = begin(group + 1) if group + 1 < groups else None
            middle_out = middle(*begun)
            if done is not None:
                finish(group - 1, *done)
            done = middle_out
            begun = following
        finish(groups - 1, *done)

    def tile_step(tile, carry):
        units = info[tile]
        for static in range(1, most + 1):
            pl.when(units == static)(functools.partial(one_tile, tile, static))
        return carry

    lax.fori_loop(0, tiles, tile_step, 0)
    for head in range(heads):
        cols = slice(head * HD, (head + 1) * HD)
        dk = dk_acc[head] * inv_root
        dv = dv_acc[head]
        own_ref[0, :, cols] = dk[front:]
        own_ref[1, :, cols] = dv[front:]
        two_ref[0, :, cols] = dk[:tok].astype(BF16)
        two_ref[1, :, cols] = dv[:tok].astype(BF16)
        one_ref[0, :, cols] = dk[tok:front].astype(BF16)
        one_ref[1, :, cols] = dv[tok:front].astype(BF16)
        k_sum = jnp.sum(dk * k_raw[head].astype(F32), axis=0, keepdims=True)
        v_sum = jnp.sum(dv * v_raw[head].astype(F32), axis=0, keepdims=True)
        for copy in range(sums_ref.shape[0]):
            sums_ref[copy, head, 0:1, :] = k_sum
            sums_ref[copy, head, 1:2, :] = v_sum


def attend(info, dstart, kscale, vscale, q, g, k_own, v_own, *received):
    tok, width = k_own.shape
    span = (REACH + 1) * tok
    tiles = tok // QT
    heads = width // HD
    step = HEADS_STEP * HD

    def at(columns):
        return pl.BlockSpec((tok, columns), lambda h: (0, h))

    pair = pl.BlockSpec((2, tok, step), lambda h: (0, 0, h))
    vec = pl.BlockSpec((1, step), lambda h: (0, h))
    group = at(q.shape[1] * step // width)
    out_shape = (
        jax.ShapeDtypeStruct(q.shape, BF16),
        jax.ShapeDtypeStruct((2, tok, width), F32),
        jax.ShapeDtypeStruct((2, tok, width), BF16),
        jax.ShapeDtypeStruct((2, tok, width), BF16),
        jax.ShapeDtypeStruct((8, heads, 2, HD), F32),
    )
    window = pltpu.VMEM((HEADS_STEP, span, HD), BF16)
    total = pltpu.VMEM((HEADS_STEP, span, HD), F32)
    return pl.pallas_call(
        attend_kernel,
        grid=(heads // HEADS_STEP,),
        in_specs=[
            pl.BlockSpec(memory_space=pltpu.SMEM),
            pl.BlockSpec((tiles, LANES), lambda h: (0, 0)),
            vec,
            vec,
            group,
            group,
        ]
        + [at(step)] * 8,
        out_specs=(
            group,
            pair,
            pair,
            pair,
            pl.BlockSpec((8, HEADS_STEP, 2, HD), lambda h: (0, h, 0, 0)),
        ),
        out_shape=out_shape,
        scratch_shapes=[
            pltpu.VMEM((tiles, REACH * tok + QT, LANES), F32),
            window,
            window,
            window,
            window,
            total,
            total,
        ],
        compiler_params=pltpu.CompilerParams(vmem_limit_bytes=58 * 2**20),
        cost_estimate=pl.CostEstimate(
            flops=heads * 8 * 256 * 576 * 128 * 10, bytes_accessed=heads * 2**21, transcendentals=0
        ),
    )(info, dstart, kscale, vscale, q, g, k_own, v_own, *received)


def finish_kernel(even_ref, kscale, vscale, own, swapped, back, gk_ref, gv_ref):
    even = even_ref[0] == 0
    for half, (out, scale) in enumerate(((gk_ref, kscale), (gv_ref, vscale))):
        near = jnp.where(even, swapped[half].astype(F32), 0.0)
        total = own[half] + near + back[half].astype(F32)
        out[...] = (total * scale[...]).astype(BF16)


def finish(parity, kscale, vscale, own, swapped, back):
    _, tok, width = own.shape
    step = 2 * HD
    pair = pl.BlockSpec((2, tok, step), lambda i: (0, 0, i))
    vec = pl.BlockSpec((1, step), lambda i: (0, i))
    out = pl.BlockSpec((tok, step), lambda i: (0, i))
    return pl.pallas_call(
        finish_kernel,
        grid=(width // step,),
        in_specs=[pl.BlockSpec(memory_space=pltpu.SMEM), vec, vec, pair, pair, pair],
        out_specs=(out, out),
        out_shape=(jax.ShapeDtypeStruct((tok, width), BF16),) * 2,
        compiler_params=pltpu.CompilerParams(vmem_limit_bytes=58 * 2**20),
    )(parity[None], kscale, vscale, own, swapped, back)


def spread_sum(copies, axis, groups):
    return jnp.sum(lax.all_to_all(copies, axis, 0, 0, axis_index_groups=groups), axis=0)


def repeated(value, count):
    return jnp.broadcast_to(value[None], (count,) + value.shape)


def body(queries, key_base, value_base, out_grad, doc_lengths, key_scale, value_scale):
    tok = queries.shape[1]
    size = lax.axis_size("seq")
    heads = key_base.shape[2] // HD
    group = queries.shape[2] // heads
    k_own = key_base[0]
    v_own = value_base[0]
    to_odd = [(i, i + 1) for i in range(0, size, 2)]
    to_even = [(i + 1, i) for i in range(0, size, 2)]
    forward = [(i, i + 2) for i in range(size - 2)]
    backward = [(i + 2, i) for i in range(size - 2)]
    device_pos = lax.axis_index("seq")
    parity = device_pos % 2

    far_k = lax.ppermute(k_own, "seq", forward)
    far_v = lax.ppermute(v_own, "seq", forward)
    near_ka = lax.ppermute(k_own, "seq", to_odd)
    near_va = lax.ppermute(v_own, "seq", to_odd)
    near_kb = lax.ppermute(far_k, "seq", to_even)
    near_vb = lax.ppermute(far_v, "seq", to_even)

    lengths = doc_lengths[0]
    starts = jnp.cumsum(lengths) - lengths
    first_key = (device_pos - REACH) * tok
    q_pos = device_pos * tok + jnp.arange(tok, dtype=jnp.int32)
    doc_start = jnp.max(jnp.where(starts[None, :] <= q_pos[:, None], starts[None, :], 0), axis=1)
    rel = (doc_start - first_key).reshape(tok // QT, QT)
    ends = REACH * tok + (jnp.arange(tok // QT, dtype=jnp.int32) + 1) * QT
    units = jnp.clip((ends - rel[:, 0] + KG - 1) // KG, 1, (DOC_MOST + QT) // KG)
    info = jnp.concatenate([units, parity[None]]).astype(jnp.int32)
    dstart = jnp.tile(rel, (1, LANES // QT))

    dq, own, two_back, one_back, sums = attend(
        info, dstart, key_scale[None], value_scale[None], queries[0], out_grad[0],
        k_own, v_own, far_k, far_v, near_ka, near_va, near_kb, near_vb,
    )
    rows = [[a * 8 + b for b in range(8)] for a in range(size // 8)]
    columns = [[a * 8 + b for a in range(size // 8)] for b in range(8)]
    partial = spread_sum(sums, "seq", rows)
    partial, one_back = lax.optimization_barrier((partial, one_back))
    swapped = lax.ppermute(one_back, "seq", to_odd + to_even)
    partial = spread_sum(repeated(partial, 4), "grp", None)
    partial, swapped = lax.optimization_barrier((partial, swapped))
    swapped_odd = jnp.where(parity == 1, swapped.astype(F32), 0.0)
    joined = (two_back.astype(F32) + swapped_odd).astype(BF16)
    back = lax.ppermute(joined, "seq", backward)
    partial, joined = lax.optimization_barrier((partial, joined))
    totals = spread_sum(repeated(partial, 8), "seq", columns)
    totals, back = lax.optimization_barrier((totals, back))
    grad_key_base, grad_value_base = finish(
        parity, key_scale[None], value_scale[None], own, swapped, back
    )
    norm = math.sqrt(lax.axis_size("grp") * size * tok)
    return (
        dq[None],
        grad_key_base[None],
        grad_value_base[None],
        totals[:, 0].reshape(heads * HD) / norm,
        totals[:, 1].reshape(heads * HD) / norm,
    )


def solution(mesh):
    return jax.shard_map(
        body,
        mesh=mesh,
        in_specs=(
            P("grp", "seq", None),
            P("grp", "seq", None),
            P("grp", "seq", None),
            P("grp", "seq", None),
            P("grp", None),
            P(),
            P(),
        ),
        out_specs=(P("grp", "seq", None), P("grp", "seq", None), P("grp", "seq", None), P(), P()),
        check_vma=False,
    )
```

```python
import functools
import math

import jax
import jax.numpy as jnp
from jax import lax
from jax.experimental import pallas as pl
from jax.experimental.pallas import tpu as pltpu
from jax.sharding import PartitionSpec as P

HD = 128
REACH = 2
DOC_MOST = 512
QT = 64
KG = 64
LANES = 256
NEG = -1e30
F32 = jnp.float32
BF16 = jnp.bfloat16
NT = (((1,), (1,)), ((), ()))


def attend_kernel(
    info, dstart, kscale, vscale, q_ref, g_ref, k_own, v_own,
    far_k, far_v, near_ka, near_va, near_kb, near_vb,
    dq_ref, own_ref, two_ref, one_ref, sums_ref,
    bias, k_raw, v_raw, k_win, v_win, dk_acc, dv_acc,
):
    tok, width = k_own.shape
    heads = width // HD
    front = REACH * tok
    packed = LANES // QT
    parts = q_ref.shape[1] // width // packed
    tiles = tok // QT
    most = (DOC_MOST + QT) // KG
    inv_root = 1.0 / math.sqrt(HD)
    log2_scale = inv_root * math.log2(math.e)
    tile = pl.program_id(0)

    @pl.when(tile == 0)
    def _():
        even = info[tiles] == 0
        for head in range(heads):
            cols = slice(head * HD, (head + 1) * HD)
            k_raw[head, :tok] = far_k[:, cols]
            v_raw[head, :tok] = far_v[:, cols]
            k_raw[head, tok:front] = jnp.where(even, near_kb[:, cols], near_ka[:, cols])
            v_raw[head, tok:front] = jnp.where(even, near_vb[:, cols], near_va[:, cols])
            k_raw[head, front:] = k_own[:, cols]
            v_raw[head, front:] = v_own[:, cols]
            k_win[head] = (k_raw[head].astype(F32) * kscale[:, cols]).astype(BF16)
            v_win[head] = (v_raw[head].astype(F32) * vscale[:, cols]).astype(BF16)
        dk_acc[...] = jnp.zeros_like(dk_acc)
        dv_acc[...] = jnp.zeros_like(dv_acc)

    reach = front + QT
    k_pos = lax.broadcasted_iota(jnp.int32, (reach, LANES), 0)
    lane = lax.broadcasted_iota(jnp.int32, (reach, LANES), 1) % QT
    start = dstart[pl.ds(tile, 1), :] - tile * QT
    bias[...] = jnp.where((k_pos >= start) & (k_pos <= lane + front), 0.0, NEG)

    def one_tile(units):
        count = units * KG
        low = pl.multiple_of(front + (tile + 1) * QT - count, KG)
        rows = pl.ds(low, count)
        mask = bias[front + QT - count :, :]

        keys_ts = [k_win[h, rows, :].T for h in range(heads)]
        groups = heads * parts
        st = [dict() for _ in range(groups)]
        totals = [None] * heads

        def load(x):
            at = range(x * packed, (x + 1) * packed)
            cols = [slice(c * HD, (c + 1) * HD) for c in at]
            st[x]["q"] = jnp.concatenate([q_ref[:, c] for c in cols], axis=0)
            st[x]["g"] = jnp.concatenate([g_ref[:, c] for c in cols], axis=0)

        def mm_s(x):
            load(x)
            st[x]["s"] = lax.dot_general(k_win[x // parts, rows, :], st[x]["q"], NT, preferred_element_type=F32)

        def mm_d(x):
            st[x]["d"] = lax.dot_general(v_win[x // parts, rows, :], st[x]["g"], NT, preferred_element_type=F32)

        def p1(x):
            st[x]["s"] = st[x]["s"] * log2_scale + mask
            st[x]["m"] = jnp.max(st[x]["s"], axis=0, keepdims=True)

        def p2(x):
            e = jnp.exp2(st[x]["s"] - st[x]["m"])
            inv = 1.0 / jnp.sum(e, axis=0, keepdims=True)
            st[x]["delta"] = jnp.sum(e * st[x]["d"], axis=0, keepdims=True) * inv
            st[x]["e"] = e
            st[x]["inv"] = inv

        def p3(x):
            w = st[x]["e"] * st[x]["inv"]
            st[x]["p"] = w.astype(BF16)
            st[x]["t"] = (w * (st[x]["d"] - st[x]["delta"])).astype(BF16)

        def mm_v(x):
            st[x]["dv"] = jnp.dot(st[x]["p"], st[x]["g"], preferred_element_type=F32)

        def mm_k(x):
            st[x]["dk"] = jnp.dot(st[x]["t"], st[x]["q"], preferred_element_type=F32)

        def mm_q(x):
            dq_t = jnp.dot(keys_ts[x // parts], st[x]["t"], preferred_element_type=F32) * inv_root
            dq = dq_t.T.astype(BF16)
            for i in range(packed):
                c = (x * packed + i) * HD
                dq_ref[:, c : c + HD] = dq[i * QT : (i + 1) * QT]

        def acc(x):
            head = x // parts
            dk, dv = st[x]["dk"], st[x]["dv"]
            if totals[head] is not None:
                dk = dk + totals[head][0]
                dv = dv + totals[head][1]
            totals[head] = (dk, dv)
            if x % parts == parts - 1:
                dk_acc[head, rows, :] += dk
                dv_acc[head, rows, :] += dv

        for turn in range(-1, groups + 2):
            for name, x in ((mm_s, turn + 1), (mm_k, turn - 2), (p2, turn), (mm_d, turn + 1), (mm_q, turn - 2), (acc, turn - 2), (p1, turn + 1), (p3, turn - 1), (mm_v, turn - 1)):
                if 0 <= x < groups:
                    name(x)

    for static in range(1, most + 1):
        pl.when(info[tile] == static)(functools.partial(one_tile, static))

    @pl.when(tile == tiles - 1)
    def _():
        for head in range(heads):
            cols = slice(head * HD, (head + 1) * HD)
            dk = dk_acc[head] * inv_root
            dv = dv_acc[head]
            own_ref[0, :, cols] = dk[front:]
            own_ref[1, :, cols] = dv[front:]
            two_ref[0, :, cols] = dk[:tok].astype(BF16)
            two_ref[1, :, cols] = dv[:tok].astype(BF16)
            one_ref[0, :, cols] = dk[tok:front].astype(BF16)
            one_ref[1, :, cols] = dv[tok:front].astype(BF16)
            k_sum = jnp.sum(dk * k_raw[head].astype(F32), axis=0, keepdims=True)
            v_sum = jnp.sum(dv * v_raw[head].astype(F32), axis=0, keepdims=True)
            for copy in range(sums_ref.shape[0]):
                sums_ref[copy, head, 0:1, :] = k_sum
                sums_ref[copy, head, 1:2, :] = v_sum


def attend(info, dstart, kscale, vscale, q, g, k_own, v_own, *received):
    tok, width = k_own.shape
    span = (REACH + 1) * tok
    tiles = tok // QT
    heads = width // HD

    def whole(*shape):
        return pl.BlockSpec(shape, lambda j: (0,) * len(shape))

    strip = pl.BlockSpec((QT, q.shape[1]), lambda j: (j, 0))
    vec = whole(1, width)
    pair = whole(2, tok, width)
    out_shape = (
        jax.ShapeDtypeStruct(q.shape, BF16),
        jax.ShapeDtypeStruct((2, tok, width), F32),
        jax.ShapeDtypeStruct((2, tok, width), BF16),
        jax.ShapeDtypeStruct((2, tok, width), BF16),
        jax.ShapeDtypeStruct((8, heads, 2, HD), F32),
    )
    window = pltpu.VMEM((heads, span, HD), BF16)
    total = pltpu.VMEM((heads, span, HD), F32)
    return pl.pallas_call(
        attend_kernel,
        grid=(tiles,),
        in_specs=[
            pl.BlockSpec(memory_space=pltpu.SMEM),
            whole(tiles, LANES),
            vec,
            vec,
            strip,
            strip,
        ]
        + [whole(tok, width)] * 8,
        out_specs=(strip, pair, pair, pair, whole(8, heads, 2, HD)),
        out_shape=out_shape,
        scratch_shapes=[
            pltpu.VMEM((REACH * tok + QT, LANES), F32),
            window,
            window,
            window,
            window,
            total,
            total,
        ],
        compiler_params=pltpu.CompilerParams(vmem_limit_bytes=58 * 2**20),
        cost_estimate=pl.CostEstimate(
            flops=heads * 8 * 256 * 576 * 128 * 10, bytes_accessed=heads * 2**21, transcendentals=0
        ),
    )(info, dstart, kscale, vscale, q, g, k_own, v_own, *received)


def finish_kernel(even_ref, kscale, vscale, own, swapped, back, gk_ref, gv_ref):
    even = even_ref[0] == 0
    for half, (out, scale) in enumerate(((gk_ref, kscale), (gv_ref, vscale))):
        near = jnp.where(even, swapped[half].astype(F32), 0.0)
        total = own[half] + near + back[half].astype(F32)
        out[...] = (total * scale[...]).astype(BF16)


def finish(parity, kscale, vscale, own, swapped, back):
    _, tok, width = own.shape
    step = 2 * HD
    pair = pl.BlockSpec((2, tok, step), lambda i: (0, 0, i))
    vec = pl.BlockSpec((1, step), lambda i: (0, i))
    out = pl.BlockSpec((tok, step), lambda i: (0, i))
    return pl.pallas_call(
        finish_kernel,
        grid=(width // step,),
        in_specs=[pl.BlockSpec(memory_space=pltpu.SMEM), vec, vec, pair, pair, pair],
        out_specs=(out, out),
        out_shape=(jax.ShapeDtypeStruct((tok, width), BF16),) * 2,
        compiler_params=pltpu.CompilerParams(vmem_limit_bytes=58 * 2**20),
    )(parity[None], kscale, vscale, own, swapped, back)


def spread_sum(copies, axis, groups):
    return jnp.sum(lax.all_to_all(copies, axis, 0, 0, axis_index_groups=groups), axis=0)


def repeated(value, count):
    return jnp.broadcast_to(value[None], (count,) + value.shape)


def body(queries, key_base, value_base, out_grad, doc_lengths, key_scale, value_scale):
    tok = queries.shape[1]
    size = lax.axis_size("seq")
    heads = key_base.shape[2] // HD
    group = queries.shape[2] // heads
    k_own = key_base[0]
    v_own = value_base[0]
    to_odd = [(i, i + 1) for i in range(0, size, 2)]
    to_even = [(i + 1, i) for i in range(0, size, 2)]
    forward = [(i, i + 2) for i in range(size - 2)]
    backward = [(i + 2, i) for i in range(size - 2)]
    device_pos = lax.axis_index("seq")
    parity = device_pos % 2

    far_k = lax.ppermute(k_own, "seq", forward)
    far_v = lax.ppermute(v_own, "seq", forward)
    near_ka = lax.ppermute(k_own, "seq", to_odd)
    near_va = lax.ppermute(v_own, "seq", to_odd)
    near_kb = lax.ppermute(far_k, "seq", to_even)

    lengths = doc_lengths[0]
    starts = jnp.cumsum(lengths) - lengths
    first_key = (device_pos - REACH) * tok
    q_pos = device_pos * tok + jnp.arange(tok, dtype=jnp.int32)
    doc_start = jnp.max(jnp.where(starts[None, :] <= q_pos[:, None], starts[None, :], 0), axis=1)
    rel = (doc_start - first_key).reshape(tok // QT, QT)
    ends = REACH * tok + (jnp.arange(tok // QT, dtype=jnp.int32) + 1) * QT
    units = jnp.clip((ends - rel[:, 0] + KG - 1) // KG, 1, (DOC_MOST + QT) // KG)
    info = jnp.concatenate([units, parity[None]]).astype(jnp.int32)
    dstart = jnp.tile(rel, (1, LANES // QT))

    far_v, near_kb, info, dstart = lax.optimization_barrier((far_v, near_kb, info, dstart))
    near_vb = lax.ppermute(far_v, "seq", to_even)
    dq, own, two_back, one_back, sums = attend(
        info, dstart, key_scale[None], value_scale[None], queries[0], out_grad[0],
        k_own, v_own, far_k, far_v, near_ka, near_va, near_kb, near_vb,
    )
    rows = [[a * 8 + b for b in range(8)] for a in range(size // 8)]
    columns = [[a * 8 + b for a in range(size // 8)] for b in range(8)]
    swapped = lax.ppermute(one_back, "seq", to_odd + to_even)
    partial = spread_sum(sums, "seq", rows)
    partial, swapped, two_back = lax.optimization_barrier((partial, swapped, two_back))
    swapped_odd = jnp.where(parity == 1, swapped.astype(F32), 0.0)
    joined = (two_back.astype(F32) + swapped_odd).astype(BF16)
    back = lax.ppermute(joined, "seq", backward)
    partial, joined = lax.optimization_barrier((partial, joined))
    partial = spread_sum(repeated(partial, 4), "grp", None)
    totals = spread_sum(repeated(partial, 8), "seq", columns)
    totals, back = lax.optimization_barrier((totals, back))
    grad_key_base, grad_value_base = finish(
        parity, key_scale[None], value_scale[None], own, swapped, back
    )
    norm = math.sqrt(lax.axis_size("grp") * size * tok)
    return (
        dq[None],
        grad_key_base[None],
        grad_value_base[None],
        totals[:, 0].reshape(heads * HD) / norm,
        totals[:, 1].reshape(heads * HD) / norm,
    )


def solution(mesh):
    return jax.shard_map(
        body,
        mesh=mesh,
        in_specs=(
            P("grp", "seq", None),
            P("grp", "seq", None),
            P("grp", "seq", None),
            P("grp", "seq", None),
            P("grp", None),
            P(),
            P(),
        ),
        out_specs=(P("grp", "seq", None), P("grp", "seq", None), P("grp", "seq", None), P(), P()),
        check_vma=False,
    )
```
